768 devices in a mesh: grp: 24 (over z, core), peer: 32 (over y, x).
Axes of the slice: x: 4, y: 8, z: 12, core: 2. Of those that a mesh axis runs over, the one named last changes fastest.
Arguments:
- grads: bfloat16 [393216, 512], P(('grp', 'peer')), may hold values from -1.796875 to 1.796875
- send_slot: int32 [768, 512], P(('grp', 'peer')), may hold values from 0 to 1535, as said below
- recv_row: int32 [768, 1536], P(('grp', 'peer')), may hold values from 0 to 768, as said below
- table: float32 [589824, 512], P(('grp', 'peer')), may hold values from -1.2 to 1.2
- accum: float32 [589824], P(('grp', 'peer')), may hold values from 0.05 to 2
Outputs:
- new_table: float32 [589824, 512], P(('grp', 'peer'))
- new_accum: float32 [589824], P(('grp', 'peer'))
- returned: bfloat16 [393216, 512], P(('grp', 'peer'))
The draws below stay inside these ranges and needn't reach their ends.
Inputs may be any that keep to these rules, and one draw needn't show every extreme that they name: Within one device the slots are distinct; send_slot // 2 is the owning device's index over grp+peer. Some 64 owners receive 2 rows from every device. recv_row[o, s * 2 + c] is the local row of owner o updated by the row that device s placed in slot o * 2 + c, and equals 768 exactly where device s placed no row there. Rows from one device to one owner are distinct; different devices may name the same row.
All inputs are finite; a program needn't handle non-finite values.
Results may differ from the reference program's by a relative error of at most 0.001.
Values may be sent and summed in bfloat16 or wider, within the bound.
A program may use at most 32 MiB of HBM per device.

```python
import math
import jax
import jax.numpy as jnp
from jax import lax

D = 512
ROWS_DEV = 768
G_DEV = 512
OWNERS = 768
CAP = 2
HOT = 64
ROWS = 589824
G_TOTAL = 393216
N_GRP = 24
N_PEER = 32


def make_plan(key):
    subkeys = jax.random.split(key, 8)
    slot_count = OWNERS * CAP
    owner_iota = jnp.arange(OWNERS, dtype=jnp.int32)
    hot_order = jnp.argsort(jax.random.randint(subkeys[0], (OWNERS,), 0, 2 ** 20) * 1024 + owner_iota, stable=True)
    hot_rank = jnp.argsort(hot_order, stable=True)
    is_hot = (hot_rank < HOT).astype(jnp.int32)
    slot_iota = jnp.arange(slot_count, dtype=jnp.int32)
    slot_hot = is_hot[slot_iota // CAP]
    scores = (slot_hot[None, :] * 2 ** 15 + jax.random.randint(subkeys[1], (OWNERS, slot_count), 0, 2 ** 14)) * 2048 + slot_iota[None, :]
    chosen = lax.top_k(scores, G_DEV)[1].astype(jnp.int32)
    shuffle = jnp.argsort(jax.random.randint(subkeys[2], (OWNERS, G_DEV), 0, 2 ** 20) * 1024 + jnp.arange(G_DEV, dtype=jnp.int32)[None, :], axis=1, stable=True)
    send_slot = jnp.take_along_axis(chosen, shuffle, axis=1)
    occupied = jnp.zeros((OWNERS, slot_count), jnp.int32).at[owner_iota[:, None], chosen].set(1)
    coin_flip = jax.random.randint(subkeys[3], (OWNERS, OWNERS), 0, 2)
    pooled = jax.random.randint(subkeys[4], (OWNERS, OWNERS), 0, 8)
    anywhere = jax.random.randint(subkeys[5], (OWNERS, OWNERS), 0, ROWS_DEV)
    offset = jax.random.randint(subkeys[6], (OWNERS,), 0, ROWS_DEV)
    first_row = jnp.where(coin_flip == 0, (offset[None, :] + pooled) % ROWS_DEV, anywhere)
    stride = jax.random.randint(subkeys[7], (OWNERS, OWNERS), 1, ROWS_DEV // CAP + 1)
    row_table = (first_row[:, :, None] + jnp.arange(CAP, dtype=jnp.int32)[None, None, :] * stride[:, :, None]) % ROWS_DEV
    row_table = jnp.where(occupied.reshape(OWNERS, OWNERS, CAP) == 1, row_table, ROWS_DEV)
    recv_row = jnp.transpose(row_table, (1, 0, 2)).reshape(OWNERS, slot_count)
    return (send_slot.astype(jnp.int32), recv_row.astype(jnp.int32))


def draw_send_slot(key, part):
    return make_plan(key)[0]


def draw_recv_row(key, part):
    return make_plan(key)[1]


def levels(rng, dims, pieces, low, top_value):
    def one(dim, blocks):
        draws = jax.random.uniform(jax.random.fold_in(jax.random.fold_in(rng, 6), dim), (blocks,), jnp.float32, low / len(pieces), top_value / len(pieces))
        return jnp.repeat(jnp.exp(draws), dims[dim] // blocks).reshape((-1,) + (1,) * (len(dims) - dim - 1))

    level = one(*pieces[0])
    for cut in pieces[1:]:
        level = level * one(*cut)
    return level


def scatter_about(stream_key, extent, deviation, limit, cuts=(), held_as=jnp.bfloat16):
    gain = levels(stream_key, extent, cuts, -0.22, 0.18) if cuts else 1.0
    entries = jax.random.normal(stream_key, extent, jnp.float32) * deviation * gain
    return jnp.minimum(jnp.maximum(entries, -limit), limit).astype(held_as)


def setup_inputs(seed: int = 0) -> dict:
    arg_keys = jax.random.split(jax.random.key(seed), 6)
    grads = scatter_about(arg_keys[0], (G_TOTAL, D), 0.3, 1.796875, ((0, 768),))
    send_slot = draw_send_slot(jax.random.fold_in(arg_keys[5], 71), 0)
    recv_row = draw_recv_row(jax.random.fold_in(arg_keys[5], 71), 0)
    table = scatter_about(arg_keys[3], (ROWS, D), 0.2, 1.2, ((0, 768),), jnp.float32)
    accum = jnp.clip(jnp.exp(math.log(2.0) - 3.6888794 * jax.random.uniform(arg_keys[4], (ROWS,), jnp.float32) ** levels(arg_keys[4], (ROWS,), ((0, 768),), -0.2, 0.2)), 0.05, 2.0)
    return {"grads": grads, "send_slot": send_slot, "recv_row": recv_row, "table": table, "accum": accum}


LEARN_RATE = 0.1
EPSILON = 1e-08

def reference(grads, send_slot, recv_row, table, accum):
    slot_cap = recv_row.shape[1] // OWNERS
    owner = (send_slot // slot_cap).astype(jnp.int32)
    sender = jnp.arange(OWNERS, dtype=jnp.int32)[:, None]
    position = (sender * slot_cap + send_slot % slot_cap).astype(jnp.int32)
    local_row = recv_row[owner, position]
    global_row = (owner * ROWS_DEV + local_row).reshape(-1).astype(jnp.int32)
    wide = grads.astype(jnp.float32)
    block_rows = N_PEER * ROWS_DEV

    def group_update(group):
        shifted = global_row - group * block_rows
        inside = (shifted >= 0) & (shifted < block_rows)
        target = jnp.where(inside, shifted, block_rows).astype(jnp.int32)
        summed = jax.ops.segment_sum(wide, target, num_segments=block_rows + 1)[:block_rows]
        start = (group * block_rows).astype(jnp.int32)
        old_table = lax.dynamic_slice_in_dim(table, start, block_rows, 0)
        old_accum = lax.dynamic_slice_in_dim(accum, start, block_rows, 0)
        fresh_accum = old_accum + lax.optimization_barrier(jnp.mean(summed * summed, axis=1))
        fresh_rows = old_table - LEARN_RATE * summed / (jnp.sqrt(fresh_accum) + EPSILON)[:, None]
        return (fresh_rows, fresh_accum)
    fresh_rows, fresh_accum = lax.map(group_update, jnp.arange(N_GRP, dtype=jnp.int32))
    new_table = fresh_rows.reshape(table.shape)
    new_accum = fresh_accum.reshape(-1)
    returned = new_table.astype(jnp.bfloat16)[global_row]
    return (new_table, new_accum, returned)
```

```python
import functools

import jax
import jax.numpy as jnp
from jax import lax
from jax.experimental import pallas as pl
from jax.experimental.pallas import tpu as pltpu
from jax.sharding import PartitionSpec as P

LEARN_RATE = 0.1
EPSILON = 1e-08
MESH = pl.DeviceIdType.MESH
CORES = 2


def update_kernel(
    n_grp, n_peer,
    grads, slot_row, slot_col, recv_row, recv_col, table, accum,
    new_table, new_accum, returned,
    out, arrived, answers, back, total, fresh, send_sem, recv_sem, send2_sem, recv2_sem, ready_sem,
):
    grp, peer = lax.axis_index("grp"), lax.axis_index("peer")
    n_z = n_grp // CORES
    z, core = grp // CORES, lax.rem(grp, CORES)
    me = grp * n_peer + peer
    plane = CORES * n_peer
    here = core * n_peer + peer
    slots = 2 * plane
    rows, width = table.shape
    count = grads.shape[0]

    barrier = pltpu.get_barrier_semaphore()

    def greet_grp(i, carry):
        pl.semaphore_signal(
            barrier, inc=1, device_id=(lax.rem(grp + i, n_grp), peer), device_id_type=MESH
        )
        return carry

    def greet_peer(i, carry):
        pl.semaphore_signal(
            barrier, inc=1, device_id=(grp, lax.rem(peer + i, n_peer)), device_id_type=MESH
        )
        return carry

    def confirm_peer(i, carry):
        pl.semaphore_signal(
            ready_sem, inc=1, device_id=(grp, lax.rem(peer + i, n_peer)), device_id_type=MESH
        )
        return carry

    lax.fori_loop(1, n_grp, greet_grp, 0)
    lax.fori_loop(1, n_peer, greet_peer, 0)
    pl.semaphore_wait(barrier, n_grp + n_peer - 2)
    lax.fori_loop(1, n_peer, confirm_peer, 0)
    pl.semaphore_wait(ready_sem, n_peer - 1)

    half = n_z // 2

    def far(step):
        return n_z - step if step else half

    def planes_to(step):
        return lax.rem(z + step, n_z), lax.rem(z + far(step), n_z)

    def planes_from(step):
        return lax.rem(z + n_z - step, n_z), lax.rem(z + n_z - far(step), n_z)

    def send(src, dst, to, s_sem, r_sem, i):
        spot = lax.rem(here + i, plane)
        pltpu.make_async_remote_copy(
            src_ref=src.at[to * plane + spot],
            dst_ref=dst.at[me],
            send_sem=s_sem,
            recv_sem=r_sem,
            device_id=(to * CORES + spot // n_peer, lax.rem(spot, n_peer)),
            device_id_type=MESH,
        ).start()

    def exchange(step, build, src, dst, s_sem, r_sems):
        first, second = planes_to(step)
        for to in (first, second):
            src[pl.ds(to * plane, plane)] = build(to).astype(jnp.bfloat16).reshape(plane, 2, width)
        sem_a, sem_b = r_sems.at[2 * step], r_sems.at[2 * step + 1]

        def both(i, carry):
            send(src, dst, first, s_sem, sem_a, i)
            send(src, dst, second, s_sem, sem_b, i)
            return carry

        if step == 0:
            pltpu.make_async_copy(src.at[me], dst.at[me], sem_a).start()
        else:
            send(src, dst, first, s_sem, sem_a, 0)
        send(src, dst, second, s_sem, sem_b, 0)
        lax.fori_loop(1, plane, both, 0)

    def collect(step, use, dst, r_sems):
        for k, src_z in enumerate(planes_from(step)):
            block = dst.at[pl.ds(src_z * plane, plane)]
            pltpu.make_async_copy(block, block, r_sems.at[2 * step + k]).wait()
            use(src_z, block[...].reshape(slots, width))

    def build_out(to):
        spot = lax.broadcasted_iota(jnp.int32, (slots, count), 0) + to * slots
        pick = (spot == slot_row[...]).astype(jnp.bfloat16)
        return jnp.dot(pick, grads[...], preferred_element_type=jnp.float32)

    for step in range(half):
        exchange(step, build_out, out, arrived, send_sem, recv_sem)

    total[...] = jnp.zeros_like(total)

    def add_block(src_z, block):
        ids = recv_row[:, pl.ds(pl.multiple_of(src_z * slots, slots), slots)]
        pick = (lax.broadcasted_iota(jnp.int32, (rows, slots), 0) == ids).astype(jnp.bfloat16)
        total[...] += jnp.dot(pick, block, preferred_element_type=jnp.float32)

    for step in range(half):
        collect(step, add_block, arrived, recv_sem)

    gsum = total[...]
    fresh_accum = accum[...] + jnp.sum(gsum * gsum, axis=1, keepdims=True) * (1.0 / width)
    new_accum[...] = fresh_accum
    updated = table[...] - LEARN_RATE * gsum / (jnp.sqrt(fresh_accum) + EPSILON)
    new_table[...] = updated
    fresh[...] = updated.astype(jnp.bfloat16)

    def build_back(to):
        ids = recv_col[pl.ds(pl.multiple_of(to * slots, slots), slots), :]
        pick = (lax.broadcasted_iota(jnp.int32, (slots, rows), 1) == ids).astype(jnp.bfloat16)
        return jnp.dot(pick, fresh[...], preferred_element_type=jnp.float32)

    for step in range(half):
        exchange(step, build_back, answers, back, send2_sem, recv2_sem)

    total[pl.ds(0, count), :] = jnp.zeros((count, width), jnp.float32)

    def place_block(src_z, block):
        spot = lax.broadcasted_iota(jnp.int32, (count, slots), 1) + src_z * slots
        pick = (spot == slot_col[...]).astype(jnp.bfloat16)
        total[pl.ds(0, count), :] += jnp.dot(pick, block, preferred_element_type=jnp.float32)

    for step in range(half):
        collect(step, place_block, back, recv2_sem)
    returned[...] = total[pl.ds(0, count), :].astype(jnp.bfloat16)

    others = n_grp * n_peer - 1
    for src, sem in ((out, send_sem), (answers, send2_sem)):
        sent = src.at[pl.ds(0, others)]
        pltpu.make_async_copy(sent, sent, sem).wait()


def per_device(grads, send_slot, recv_row, table, accum):
    n_grp, n_peer = lax.axis_size("grp"), lax.axis_size("peer")
    devices = n_grp * n_peer
    count, width = grads.shape
    rows = table.shape[0]
    slot_count = recv_row.shape[1]
    vmem = pl.BlockSpec(memory_space=pltpu.VMEM)
    blocks = pltpu.VMEM((devices, 2, width), jnp.bfloat16)
    n_z = n_grp // CORES
    new_table, new_accum, returned = pl.pallas_call(
        functools.partial(update_kernel, n_grp, n_peer),
        out_shape=(
            jax.ShapeDtypeStruct((rows, width), jnp.float32),
            jax.ShapeDtypeStruct((rows, 1), jnp.float32),
            jax.ShapeDtypeStruct((count, width), jnp.bfloat16),
        ),
        in_specs=[vmem] * 7,
        out_specs=(vmem, vmem, vmem),
        scratch_shapes=[
            blocks, blocks, blocks, blocks,
            pltpu.VMEM((rows, width), jnp.float32),
            pltpu.VMEM((rows, width), jnp.bfloat16),
            pltpu.SemaphoreType.DMA,
            pltpu.SemaphoreType.DMA((n_z,)),
            pltpu.SemaphoreType.DMA,
            pltpu.SemaphoreType.DMA((n_z,)),
            pltpu.SemaphoreType.REGULAR,
        ],
        compiler_params=pltpu.CompilerParams(
            collective_id=0, has_side_effects=True, vmem_limit_bytes=48 * 2**20
        ),
    )(
        grads, send_slot, send_slot.reshape(count, 1), recv_row,
        recv_row.reshape(slot_count, 1), table, accum.reshape(rows, 1),
    )
    return new_table, new_accum.reshape(rows), returned


def solution(mesh):
    rows = P(("grp", "peer"), None)
    return jax.shard_map(
        per_device,
        mesh=mesh,
        in_specs=(rows, rows, rows, rows, P(("grp", "peer"))),
        out_specs=(rows, P(("grp", "peer")), rows),
        check_vma=False,
    )
```

```python
import functools

import jax
import jax.numpy as jnp
from jax import lax
from jax.experimental import pallas as pl
from jax.experimental.pallas import tpu as pltpu
from jax.sharding import PartitionSpec as P

LEARN_RATE = 0.1
EPSILON = 1e-08
MESH = pl.DeviceIdType.MESH
CORES = 2
LANES = 128


def near_first(n_z):
    order = [0]
    for d in range(1, (n_z + 1) // 2):
        order += [d, n_z - d]
    return order + ([n_z // 2] if n_z % 2 == 0 else [])


def as_column(row, copies):
    return jnp.transpose(jnp.broadcast_to(row, (copies, row.shape[1])))


def update_kernel(
    n_grp, n_peer, cap,
    grads_hbm, slot_hbm, recv_hbm, table_hbm, accum_hbm,
    table_out, accum_out, returned_out, flag_out,
    grads, slot, recv, table, accum, key_row, key_col, returned,
    packed, packed_in, ids, ids_in, mid, arrived, answers, answers_in, repacked, repacked_in,
    flags, total, fresh,
    load_sem, send_sem, pack_sem, ids_sem, row_sem, flag_sem, answer_sem, back_sem, store_sem,
):
    grp, peer = lax.axis_index("grp"), lax.axis_index("peer")
    n_z = n_grp // CORES
    z, core = grp // CORES, lax.rem(grp, CORES)
    plane = CORES * n_peer
    here = core * n_peer + peer
    slots = 2 * plane
    rows, width = table.shape
    count = grads.shape[0]
    order = near_first(n_z)

    loads = [
        pltpu.make_async_copy(src, dst, load_sem.at[i])
        for i, (src, dst) in enumerate(
            ((slot_hbm, slot), (grads_hbm, grads), (recv_hbm, recv), (accum_hbm, accum), (table_hbm, table))
        )
    ]
    for load in loads:
        load.start()

    barrier = pltpu.get_barrier_semaphore()

    def at_place(spot):
        return (z * CORES + spot // n_peer, lax.rem(spot, n_peer))

    def greet_line(i, carry):
        there = lax.rem(z + i, n_z) * CORES + core
        pl.semaphore_signal(barrier, inc=1, device_id=(there, peer), device_id_type=MESH)
        return carry

    def greet_plane(i, carry):
        pl.semaphore_signal(
            barrier, inc=1, device_id=at_place(lax.rem(here + i, plane)), device_id_type=MESH
        )
        return carry

    lax.fori_loop(1, n_z, greet_line, 0)
    lax.fori_loop(1, plane, greet_plane, 0)

    loads[0].wait()
    goal = lax.div(slot[...], slots)
    member = (lax.broadcasted_iota(jnp.int32, (-(-n_z // 16) * 16, count), 0) == goal)
    before = lax.broadcasted_iota(jnp.int32, (count, count), 0) < lax.broadcasted_iota(
        jnp.int32, (count, count), 1
    )
    ranks = jnp.dot(
        member.astype(jnp.bfloat16), before.astype(jnp.bfloat16), preferred_element_type=jnp.float32
    )
    rank = jnp.sum(jnp.where(member, ranks, 0.0), axis=0, keepdims=True).astype(jnp.int32)
    key_row[...] = jnp.where(rank < cap, goal * LANES + rank, -1)
    key_col[...] = as_column(key_row[...], LANES)
    over = jnp.max(jnp.where(rank < cap, 0.0, 1.0), axis=1, keepdims=True)
    place = (slot[...] - goal * slots + 1).astype(jnp.float32).astype(jnp.bfloat16)
    place = jnp.broadcast_to(place, (16, count))
    last_lane = lax.broadcasted_iota(jnp.int32, (8, LANES), 1) == LANES - 1

    loads[1].wait()
    pl.semaphore_wait(barrier, n_z + plane - 2)

    def line_copy(src, dst, sem, to):
        return pltpu.make_async_remote_copy(
            src_ref=src, dst_ref=dst, send_sem=send_sem.at[0], recv_sem=sem,
            device_id=(to * CORES + core, peer), device_id_type=MESH,
        )

    for k in order:
        to = lax.rem(z + k, n_z)
        pick = lax.broadcasted_iota(jnp.int32, (LANES, count), 0) + to * LANES == key_row[...]
        pick = pick.astype(jnp.bfloat16)
        block = jnp.dot(pick[:cap], grads[...], preferred_element_type=jnp.float32)
        names = lax.dot_general(
            place, pick, (((1,), (1,)), ((), ())), preferred_element_type=jnp.float32
        )
        names = jnp.where(last_lane, over, names[:8])
        if k == 0:
            packed_in[0] = block.astype(jnp.bfloat16)
            ids_in[0] = names
        else:
            packed[k] = block.astype(jnp.bfloat16)
            ids[k] = names
            line_copy(packed.at[k], packed_in.at[k], pack_sem.at[k], to).start()
            line_copy(ids.at[k], ids_in.at[k], ids_sem.at[k], to).start()

    def spread_plane(src, dst, sem, k):
        def one(i, carry):
            spot = lax.rem(here + i, plane)
            pltpu.make_async_remote_copy(
                src_ref=src.at[k * plane + spot],
                dst_ref=dst.at[k * plane + here],
                send_sem=send_sem.at[1],
                recv_sem=sem.at[k],
                device_id=at_place(spot),
                device_id_type=MESH,
            ).start()
            return carry

        mine = k * plane + here
        pltpu.make_async_copy(src.at[mine], dst.at[mine], sem.at[k]).start()
        lax.fori_loop(1, plane, one, 0)

    def wait_plane(dst, sem, k):
        block = dst.at[pl.ds(k * plane, plane)]
        pltpu.make_async_copy(block, block, sem.at[k]).wait()
        return block[...].reshape(slots, width)

    def unpack_matrix(k):
        spot = lax.broadcasted_iota(jnp.int32, (slots, LANES), 0) + 1
        return (spot.astype(jnp.float32) == ids_in[k][0:1, :]).astype(jnp.bfloat16)

    def origin(k):
        return lax.rem(z + n_z - k, n_z)

    loads[2].wait()
    total[...] = jnp.zeros_like(total)

    def add_rows(k):
        block = wait_plane(arrived, row_sem, k)
        names = recv[:, pl.ds(pl.multiple_of(origin(k) * slots, slots), slots)]
        pick = (lax.broadcasted_iota(jnp.int32, (rows, slots), 0) == names).astype(jnp.bfloat16)
        total[...] += jnp.dot(pick, block, preferred_element_type=jnp.float32)

    lag = 2
    for i in range(n_z + lag):
        if i < n_z:
            k = order[i]
            if k:
                pltpu.make_async_copy(packed_in.at[k], packed_in.at[k], pack_sem.at[k]).wait()
                pltpu.make_async_copy(ids_in.at[k], ids_in.at[k], ids_sem.at[k]).wait()
            block = jnp.dot(
                unpack_matrix(k)[:, :cap], packed_in[k], preferred_element_type=jnp.float32
            )
            mid[pl.ds(k * plane, plane)] = block.astype(jnp.bfloat16).reshape(plane, 2, width)
            spread_plane(mid, arrived, row_sem, k)
        if i >= lag:
            add_rows(order[i - lag])

    some = jnp.max(ids_in[...], axis=0)
    some = jnp.max(jnp.where(last_lane, some, 0.0), axis=1, keepdims=True)
    flags[pl.ds(here, 1)] = jnp.broadcast_to(some, (1, 8, LANES))

    def tell(i, carry):
        pltpu.make_async_remote_copy(
            src_ref=flags.at[here], dst_ref=flags.at[here], send_sem=send_sem.at[2],
            recv_sem=flag_sem, device_id=at_place(lax.rem(here + i, plane)), device_id_type=MESH,
        ).start()
        return carry

    lax.fori_loop(1, plane, tell, 0)

    loads[3].wait()
    loads[4].wait()
    gsum = total[...]
    fresh_accum = as_column(accum[...], LANES)[:, :1] + jnp.sum(
        gsum * gsum, axis=1, keepdims=True
    ) * (1.0 / width)
    updated = table[...] - LEARN_RATE * gsum / (jnp.sqrt(fresh_accum) + EPSILON)
    fresh[...] = updated.astype(jnp.bfloat16)

    far = order[::-1]
    for i in range(n_z + lag):
        if i < n_z:
            k = far[i]
            names = recv[:, pl.ds(pl.multiple_of(origin(k) * slots, slots), slots)]
            names = as_column(names, LANES)[:, :1]
            pick = (lax.broadcasted_iota(jnp.int32, (slots, rows), 1) == names).astype(jnp.bfloat16)
            block = jnp.dot(pick, fresh[...], preferred_element_type=jnp.float32)
            answers[pl.ds(k * plane, plane)] = block.astype(jnp.bfloat16).reshape(plane, 2, width)
            spread_plane(answers, answers_in, answer_sem, k)
        if i == 0:
            table[...] = updated
            accum[...] = jnp.transpose(jnp.broadcast_to(fresh_accum, (rows, LANES)))[:1, :]
            stores = [
                pltpu.make_async_copy(table, table_out, store_sem.at[0]),
                pltpu.make_async_copy(accum, accum_out, store_sem.at[1]),
            ]
            for store in stores:
                store.start()
        if i >= lag:
            k = far[i - lag]
            block = wait_plane(answers_in, answer_sem, k)
            block = lax.dot_general(
                unpack_matrix(k), block, (((0,), (0,)), ((), ())), preferred_element_type=jnp.float32
            )
            if k == 0:
                repacked_in[0] = block[:cap].astype(jnp.bfloat16)
            else:
                repacked[k] = block[:cap].astype(jnp.bfloat16)
                line_copy(repacked.at[k], repacked_in.at[k], back_sem.at[k], origin(k)).start()

    total[pl.ds(0, count), :] = jnp.zeros((count, width), jnp.float32)
    for k in far:
        if k:
            pltpu.make_async_copy(repacked_in.at[k], repacked_in.at[k], back_sem.at[k]).wait()
        lane = lax.broadcasted_iota(jnp.int32, (count, LANES), 1) + lax.rem(z + k, n_z) * LANES
        pick = (lane == key_col[...]).astype(jnp.bfloat16)[:, :cap]
        total[pl.ds(0, count), :] += jnp.dot(
            pick, repacked_in[k], preferred_element_type=jnp.float32
        )
    returned[...] = total[pl.ds(0, count), :].astype(jnp.bfloat16)
    stores.append(pltpu.make_async_copy(returned, returned_out, store_sem.at[2]))
    stores[-1].start()

    told = flags.at[pl.ds(0, plane - 1)]
    pltpu.make_async_copy(told, told, flag_sem).wait()
    flag_out[...] = jnp.max(flags[...], axis=0)

    for k in range(1, n_z):
        for part in (packed, ids, repacked):
            pltpu.make_async_copy(part.at[k], part.at[k], send_sem.at[0]).wait()
    for part in (mid, answers):
        sent = part.at[pl.ds(0, n_z * (plane - 1))]
        pltpu.make_async_copy(sent, sent, send_sem.at[1]).wait()
    pltpu.make_async_copy(told, told, send_sem.at[2]).wait()
    for store in stores:
        store.wait()


def slow_update(grads, send_slot, recv_row, table, accum):
    n_grp, n_peer = lax.axis_size("grp"), lax.axis_size("peer")
    slot_count, width, row_count = recv_row.shape[1], grads.shape[1], table.shape[0]
    slot_cap = slot_count // (n_grp * n_peer)
    my_slots, row_ids = send_slot[0], recv_row[0]

    def exchange(blocks):
        blocks = blocks.reshape(n_grp, n_peer, slot_cap, width)
        blocks = lax.all_to_all(blocks, "grp", split_axis=0, concat_axis=0, tiled=True)
        blocks = lax.all_to_all(blocks, "peer", split_axis=1, concat_axis=1, tiled=True)
        return blocks.reshape(slot_count, width)

    arrived = exchange(jnp.zeros((slot_count, width), jnp.bfloat16).at[my_slots].set(grads))
    selector = jnp.arange(row_count, dtype=jnp.int32)[:, None] == row_ids[None, :]
    summed = jnp.dot(selector.astype(jnp.bfloat16), arrived, preferred_element_type=jnp.float32)
    new_accum = accum + jnp.mean(summed * summed, axis=1)
    new_table = table - LEARN_RATE * summed / (jnp.sqrt(new_accum) + EPSILON)[:, None]
    padded = jnp.concatenate(
        [new_table.astype(jnp.bfloat16), jnp.zeros((1, width), jnp.bfloat16)], axis=0
    )
    return new_table, new_accum, exchange(padded[row_ids])[my_slots]


def per_device(grads, send_slot, recv_row, table, accum):
    n_grp, n_peer = lax.axis_size("grp"), lax.axis_size("peer")
    count, width = grads.shape
    rows = table.shape[0]
    slot_count = recv_row.shape[1]
    devices = n_grp * n_peer
    n_z, plane = n_grp // CORES, CORES * n_peer
    slots = 2 * plane
    cap = slots * 5 // 8
    hbm = pl.BlockSpec(memory_space=pltpu.HBM)
    vmem = pl.BlockSpec(memory_space=pltpu.VMEM)
    blocks = pltpu.VMEM((devices, 2, width), jnp.bfloat16)
    packs = pltpu.VMEM((n_z, cap, width), jnp.bfloat16)
    names = pltpu.VMEM((n_z, 8, LANES), jnp.float32)
    dma = pltpu.SemaphoreType.DMA
    new_table, new_accum, returned, flag = pl.pallas_call(
        functools.partial(update_kernel, n_grp, n_peer, cap),
        out_shape=(
            jax.ShapeDtypeStruct((rows, width), jnp.float32),
            jax.ShapeDtypeStruct((1, rows), jnp.float32),
            jax.ShapeDtypeStruct((count, width), jnp.bfloat16),
            jax.ShapeDtypeStruct((8, LANES), jnp.float32),
        ),
        in_specs=[hbm] * 5,
        out_specs=(hbm, hbm, hbm, vmem),
        scratch_shapes=[
            pltpu.VMEM((count, width), jnp.bfloat16),
            pltpu.VMEM((1, count), jnp.int32),
            pltpu.VMEM((1, slot_count), jnp.int32),
            pltpu.VMEM((rows, width), jnp.float32),
            pltpu.VMEM((1, rows), jnp.float32),
            pltpu.VMEM((1, count), jnp.int32),
            pltpu.VMEM((count, LANES), jnp.int32),
            pltpu.VMEM((count, width), jnp.bfloat16),
            packs, packs, names, names, blocks, blocks, blocks, blocks, packs, packs,
            pltpu.VMEM((plane, 8, LANES), jnp.float32),
            pltpu.VMEM((rows, width), jnp.float32),
            pltpu.VMEM((rows, width), jnp.bfloat16),
            dma((5,)), dma((3,)), dma((n_z,)), dma((n_z,)), dma((n_z,)), dma, dma((n_z,)), dma((n_z,)),
            dma((3,)),
        ],
        compiler_params=pltpu.CompilerParams(
            collective_id=0, has_side_effects=True, vmem_limit_bytes=48 * 2**20
        ),
    )(grads, send_slot, recv_row, table, accum.reshape(1, rows))
    fast = (new_table, new_accum.reshape(rows), returned)
    return lax.cond(
        flag[0, 0] > 0.5,
        lambda fast, *args: slow_update(*args),
        lambda fast, *args: fast,
        fast, grads, send_slot, recv_row, table, accum,
    )


def solution(mesh):
    rows = P(("grp", "peer"), None)
    return jax.shard_map(
        per_device,
        mesh=mesh,
        in_specs=(rows, rows, rows, rows, P(("grp", "peer"))),
        out_specs=(rows, P(("grp", "peer")), rows),
        check_vma=False,
    )
```
